32 devices in a mesh: row: 16 (over z, y, x), col: 2 (over core).
Axes of the slice: x: 2, y: 2, z: 4, core: 2. Of those that a mesh axis runs over, the one named last changes fastest.
Arguments:
- orbitals: bfloat16 [4096, 2, 256], P(('row', 'col')), may hold values from -6 to 6
- kernel: bfloat16 [4096, 4096], P('row', 'col'), may hold values from -0.005859375 to 0.005859375
- basis: bfloat16 [4096, 2048], P('row'), may hold values from -0.09375 to 0.09375
Outputs:
- exchange: float32 [2048, 2, 256], P('row')
The draws below stay inside these ranges and needn't reach their ends.
All inputs are finite; a program needn't handle non-finite values.
Results may differ from the reference program's by a relative error of at most 0.0041.
Values may be sent and summed in bfloat16 or wider, within the bound.
No kernel may reach another device: no remote copies, remote signals or barrier semaphores. Data moves between devices by JAX's collectives and lax.ppermute only.
A program may use at most 64 MiB of HBM per device.

```python
import jax
import jax.numpy as jnp
from jax import lax

NOCC = 256
NBASIS = 2048
PR = 256
PIECE = 128
NPTS = 4096
N_ROW = 16
N_COL = 2


def level_of(stream_key, shape, split, least, largest):
    gain = 1.0
    for position, parts in split:
        heights = jax.random.uniform(jax.random.fold_in(jax.random.fold_in(stream_key, 6), position), (parts,), jnp.float32, least / len(split), largest / len(split))
        gain = gain * jnp.repeat(jnp.exp(heights), shape[position] // parts).reshape((-1,) + (1,) * (len(shape) - 1 - position))
    return gain


def scatter_about(rng, extent, spread, bound, shards=(), dtype=jnp.bfloat16):
    values = spread * jax.random.normal(rng, extent, jnp.float32)
    if shards:
        values = values * level_of(rng, extent, shards, -0.22, 0.18)
    return jnp.clip(values, -bound, bound).astype(dtype)


def setup_inputs(seed: int = 0) -> dict:
    key_list = jax.random.split(jax.random.key(seed), 4)
    return {
        "orbitals": scatter_about(key_list[0], (NPTS, 2, NOCC), 1.0, 6.0, ((0, 32),)),
        "kernel": scatter_about(key_list[1], (NPTS, NPTS), (NOCC * NPTS) ** -0.5, 0.005859375, ((0, 16), (1, 2))),
        "basis": scatter_about(key_list[2], (NPTS, NBASIS), NPTS ** -0.5, 0.09375, ((0, 16),)),
    }


def reference(orbitals, kernel, basis):
    values = orbitals.astype(jnp.float32)
    columns = values.reshape(N_ROW, N_COL, PIECE, 2, NOCC).transpose(1, 0, 2, 3, 4).reshape(NPTS, 2, NOCC)
    row_blocks = values.reshape(N_ROW, PR, 2, NOCC)
    kernel_blocks = kernel.reshape(N_ROW, PR, NPTS)

    def block(block_pair):
        row_values, kernel_rows = block_pair
        density = jnp.einsum("psi,qsi->spq", row_values, columns)
        weighted = (density * kernel_rows.astype(jnp.float32)[None]).astype(jnp.bfloat16)
        weighted = lax.optimization_barrier(weighted).astype(jnp.float32)
        return jnp.einsum("spq,qsi->psi", weighted, columns)

    applied = lax.map(block, (row_blocks, kernel_blocks)).reshape(NPTS, 2, NOCC)
    rounded = lax.optimization_barrier(applied.astype(jnp.bfloat16)).astype(jnp.float32)
    return jnp.einsum("pm,psi->msi", basis.astype(jnp.float32), rounded)
```

```python
import functools

import jax
import jax.numpy as jnp
from jax import lax
from jax.experimental import pallas as pl
from jax.experimental.pallas import tpu as pltpu
from jax.sharding import PartitionSpec as P

F32 = jnp.float32
BF16 = jnp.bfloat16
VMEM = pl.BlockSpec(memory_space=pltpu.VMEM)
SMEM = pl.BlockSpec(memory_space=pltpu.SMEM)
LIMIT = 40 * 1024 * 1024


def general_body(orbitals, kernel, basis):
    row_orbitals = lax.all_gather(orbitals, "col", axis=0, tiled=True)
    point_rows = row_orbitals.shape[0]
    occupied = orbitals.shape[2]
    column_orbitals = lax.all_gather(orbitals, "row", axis=0, tiled=True)
    density = jnp.einsum(
        "psi,qsi->spq", row_orbitals, column_orbitals, preferred_element_type=F32
    )
    weighted = (density * kernel[None].astype(F32)).astype(BF16)
    applied = jnp.einsum(
        "spq,qsi->psi", weighted, column_orbitals, preferred_element_type=F32
    )
    out_rows = basis.shape[1] // lax.axis_size("row")
    summed = lax.psum(applied, "col").astype(BF16)
    flattened = summed.reshape(point_rows, -1)
    result = lax.psum_scatter(
        lax.dot_general(basis, flattened, (((0,), (0,)), ((), ())), preferred_element_type=F32),
        "row",
        scatter_dimension=0,
        tiled=True,
    )
    return result.reshape(out_rows, 2, occupied)


def apply_kernel(n_parts, piece, accumulate, ids, rows, kernel_own, kernel_other, *refs):
    parts = refs[:n_parts]
    acc = refs[n_parts] if accumulate else None
    out = refs[-1]
    total = acc[...] if accumulate else None
    left = rows[...]
    block = 2 * piece
    index = 0
    for part in parts:
        for b in range(part.shape[0] // block):
            columns = part[b * block : (b + 1) * block, :]
            at = pl.ds(pl.multiple_of(ids[index] * piece, piece), piece)
            index += 1
            density = lax.dot_general(
                left, columns, (((1,), (1,)), ((), ())), preferred_element_type=F32
            )
            tile = jnp.concatenate([kernel_own[:, at], kernel_other[:, at]], axis=1)
            weighted = (density * tile.astype(F32)).astype(BF16)
            term = jnp.dot(weighted, columns, preferred_element_type=F32)
            total = term if total is None else total + term
    out[...] = total.astype(out.dtype)


def apply_blocks(ids, rows, kernel_own, kernel_other, parts, acc, dtype):
    args = [ids, rows, kernel_own, kernel_other, *parts]
    if acc is not None:
        args.append(acc)
    columns = sum(part.shape[0] for part in parts)
    n, i = rows.shape
    return pl.pallas_call(
        functools.partial(apply_kernel, len(parts), kernel_own.shape[1] // 16, acc is not None),
        out_shape=jax.ShapeDtypeStruct((n, i), dtype),
        in_specs=[SMEM] + [VMEM] * (len(args) - 1),
        out_specs=VMEM,
        compiler_params=pltpu.CompilerParams(vmem_limit_bytes=LIMIT),
        cost_estimate=pl.CostEstimate(
            flops=4 * n * i * columns, bytes_accessed=2 * columns * (n + i), transcendentals=0
        ),
    )(*args)


def project_kernel(width, ids, basis, applied, out):
    right = applied[...]
    for b in range(out.shape[0] // width):
        at = pl.ds(pl.multiple_of(ids[b] * width, width), width)
        out[b * width : (b + 1) * width, :] = lax.dot_general(
            basis[:, at], right, (((0,), (0,)), ((), ())), preferred_element_type=F32
        ).astype(out.dtype)


def project(ids, basis, applied, width, blocks, dtype):
    p, i = applied.shape
    return pl.pallas_call(
        functools.partial(project_kernel, width),
        out_shape=jax.ShapeDtypeStruct((blocks * width, i), dtype),
        in_specs=[SMEM, VMEM, VMEM],
        out_specs=VMEM,
        compiler_params=pltpu.CompilerParams(vmem_limit_bytes=LIMIT),
        cost_estimate=pl.CostEstimate(
            flops=2 * p * i * blocks * width, bytes_accessed=2 * blocks * width * (p + i), transcendentals=0
        ),
    )(ids, basis, applied)


def box_body(orbitals, kernel, basis):
    r = lax.axis_index("row")
    c = lax.axis_index("col")
    piece = orbitals.shape[0]

    def send(a, to):
        pairs = [(2 * q + k, 2 * to(q, k) + k) for q in range(16) for k in range(2)]
        return lax.ppermute(a, ("row", "col"), pairs)

    first = lambda a: send(a, lambda q, k: q ^ (1 + k))
    second = lambda a: send(a, lambda q, k: q ^ (2 - k))
    plane = lambda a, d: send(a, lambda q, k: (q + 4 * d) % 16)
    swap = lambda a: lax.ppermute(a, "col", [(0, 1), (1, 0)])
    join = lambda *a: jnp.concatenate(a, axis=0)

    own = lax.dynamic_index_in_dim(orbitals, c, 1, keepdims=False)
    other = swap(lax.dynamic_index_in_dim(orbitals, 1 - c, 1, keepdims=False))
    kernel_other = swap(kernel)
    block = join(own, other)
    rows = jnp.where(c == 0, block, join(other, own))

    near, far = 1 + c, 2 - c
    x0 = first(block)
    z1 = plane(block, 1)
    p0 = join(block, x0)
    y0 = second(p0)
    z2 = plane(z1, 1)
    zp = plane(join(p0, y0), -1)
    z12 = join(z1, z2)
    x12 = first(z12)
    y12 = second(join(z12, x12))

    up, down, twice = (r + 4) % 16, (r + 12) % 16, (r + 8) % 16
    ids = lambda *v: jnp.stack(v).astype(jnp.int32)
    acc = apply_blocks(
        ids(r, r ^ near, r ^ far, r ^ 3), rows, kernel, kernel_other, [block, x0, y0], None, F32
    )
    acc = apply_blocks(
        ids(up, up ^ near, up ^ far, up ^ 3, down, twice, down ^ near, twice ^ near),
        rows, kernel, kernel_other, [zp, z12, x12], acc, F32,
    )
    applied = apply_blocks(
        ids(down ^ far, twice ^ far, down ^ 3, twice ^ 3), rows, kernel, kernel_other, [y12], acc, BF16
    )

    width = basis.shape[1] // 16
    along = lambda base: [(base + 4 * k) % 16 for k in range(4)]
    send1 = project(ids(*along(r ^ far), *along(r ^ 3)), basis, applied, width, 8, BF16)
    keep1 = project(ids(*along(r), *along(r ^ near)), basis, applied, width, 8, F32)
    half = 4 * width
    got1 = second(send1)
    send2 = (keep1[half:] + got1[half:].astype(F32)).astype(BF16)
    keep2 = keep1[:half] + got1[:half].astype(F32)
    got2 = first(send2)
    sums = keep2 + got2.astype(F32)
    result = sums[:width]
    for k in (1, 2, 3):
        result = result + plane(sums[k * width : (k + 1) * width].astype(BF16), k).astype(F32)
    partner = swap(result)
    return jnp.where(
        c == 0, jnp.stack([result, partner], axis=1), jnp.stack([partner, result], axis=1)
    )


def solution(mesh):
    box = dict(mesh.shape) == {"row": 16, "col": 2}
    return jax.shard_map(
        box_body if box else general_body,
        mesh=mesh,
        in_specs=(P(("row", "col"), None, None), P("row", "col"), P("row", None)),
        out_specs=P("row", None, None),
        check_vma=False,
    )
```

```python
import functools

import jax
import jax.numpy as jnp
from jax import lax
from jax.experimental import pallas as pl
from jax.experimental.pallas import tpu as pltpu
from jax.sharding import PartitionSpec as P

F32 = jnp.float32
BF16 = jnp.bfloat16
VMEM = pl.BlockSpec(memory_space=pltpu.VMEM)
SMEM = pl.BlockSpec(memory_space=pltpu.SMEM)
LIMIT = 40 * 1024 * 1024


def general_body(orbitals, kernel, basis):
    row_orbitals = lax.all_gather(orbitals, "col", axis=0, tiled=True)
    point_rows = row_orbitals.shape[0]
    occupied = orbitals.shape[2]
    column_orbitals = lax.all_gather(orbitals, "row", axis=0, tiled=True)
    density = jnp.einsum(
        "psi,qsi->spq", row_orbitals, column_orbitals, preferred_element_type=F32
    )
    weighted = (density * kernel[None].astype(F32)).astype(BF16)
    applied = jnp.einsum(
        "spq,qsi->psi", weighted, column_orbitals, preferred_element_type=F32
    )
    out_rows = basis.shape[1] // lax.axis_size("row")
    summed = lax.psum(applied, "col").astype(BF16)
    flattened = summed.reshape(point_rows, -1)
    result = lax.psum_scatter(
        lax.dot_general(basis, flattened, (((0,), (0,)), ((), ())), preferred_element_type=F32),
        "row",
        scatter_dimension=0,
        tiled=True,
    )
    return result.reshape(out_rows, 2, occupied)


PARAMS = pltpu.CompilerParams(vmem_limit_bytes=LIMIT)


def tile_at(index, width):
    return pl.ds(pl.multiple_of(index * width, width), width)


def split_kernel(core, orbitals, own, other):
    first_core = core[0] == 0
    zero, one = orbitals[:, 0, :], orbitals[:, 1, :]
    own[...] = jnp.where(first_core, zero, one)
    other[...] = jnp.where(first_core, one, zero)


def split_spins(core, orbitals):
    p, _, i = orbitals.shape
    return pl.pallas_call(
        split_kernel,
        out_shape=[jax.ShapeDtypeStruct((p, i), orbitals.dtype)] * 2,
        in_specs=[SMEM, VMEM],
        out_specs=[VMEM] * 2,
        compiler_params=PARAMS,
    )(core, orbitals)


def join_kernel(*refs):
    out = refs[-1]
    start = 0
    for ref in refs[:-1]:
        out[start : start + ref.shape[0], :] = ref[...]
        start += ref.shape[0]


def join_blocks(*blocks):
    rows = sum(block.shape[0] for block in blocks)
    return pl.pallas_call(
        join_kernel,
        out_shape=jax.ShapeDtypeStruct((rows, blocks[0].shape[1]), blocks[0].dtype),
        in_specs=[VMEM] * len(blocks),
        out_specs=VMEM,
        compiler_params=PARAMS,
        cost_estimate=pl.CostEstimate(flops=2 * 10**10, bytes_accessed=10**6, transcendentals=0),
    )(*blocks)


def turn_kernel(width, ids, basis, out):
    for b in range(out.shape[0] // width):
        out[b * width : (b + 1) * width, :] = basis[:, tile_at(ids[b], width)].T


def turn_tiles(ids, basis, width):
    return pl.pallas_call(
        functools.partial(turn_kernel, width),
        out_shape=jax.ShapeDtypeStruct((ids.shape[0] * width, basis.shape[0]), basis.dtype),
        in_specs=[SMEM, VMEM],
        out_specs=VMEM,
        compiler_params=PARAMS,
    )(ids, basis)


def apply_kernel(n_parts, piece, accumulate, ids, rows, kernel_own, kernel_other, *refs):
    parts = refs[:n_parts]
    acc = refs[n_parts] if accumulate else None
    out = refs[-1]
    total = acc[...] if accumulate else None
    left = rows[...]
    block = 2 * piece
    index = 0
    for part in parts:
        for b in range(part.shape[0] // block):
            columns = part[b * block : (b + 1) * block, :]
            at = pl.ds(pl.multiple_of(ids[index] * piece, piece), piece)
            index += 1
            density = lax.dot_general(
                left, columns, (((1,), (1,)), ((), ())), preferred_element_type=F32
            )
            tile = jnp.concatenate([kernel_own[:, at], kernel_other[:, at]], axis=1)
            weighted = (density * tile.astype(F32)).astype(BF16)
            term = jnp.dot(weighted, columns, preferred_element_type=F32)
            total = term if total is None else total + term
    out[...] = total.astype(out.dtype)


def apply_blocks(ids, rows, kernel_own, kernel_other, parts, acc, dtype, weight):
    args = [ids, rows, kernel_own, kernel_other, *parts]
    if acc is not None:
        args.append(acc)
    columns = sum(part.shape[0] for part in parts)
    n, i = rows.shape
    return pl.pallas_call(
        functools.partial(apply_kernel, len(parts), kernel_own.shape[1] // 16, acc is not None),
        out_shape=jax.ShapeDtypeStruct((n, i), dtype),
        in_specs=[SMEM] + [VMEM] * (len(args) - 1),
        out_specs=VMEM,
        compiler_params=PARAMS,
        cost_estimate=pl.CostEstimate(
            flops=weight * 4 * n * i * columns, bytes_accessed=weight * 2 * columns * (n + i), transcendentals=0
        ),
    )(*args)


def project_kernel(start, tiles, applied, *outs):
    for out in outs:
        n = out.shape[0]
        total = jnp.dot(tiles[start : start + n, :], applied[...], preferred_element_type=F32)
        out[...] = total.astype(out.dtype)
        start += n


def project(start, tiles, applied, shapes):
    p, i = applied.shape
    rows = sum(n for n, _ in shapes)
    return pl.pallas_call(
        functools.partial(project_kernel, start),
        out_shape=[jax.ShapeDtypeStruct((n, i), t) for n, t in shapes],
        in_specs=[VMEM, VMEM],
        out_specs=[VMEM] * len(shapes),
        compiler_params=PARAMS,
        cost_estimate=pl.CostEstimate(flops=2 * rows * p * i, bytes_accessed=4 * rows * p, transcendentals=0),
    )(tiles, applied)


def box_body(orbitals, kernel, basis):
    r = lax.axis_index("row")
    c = lax.axis_index("col")
    piece = orbitals.shape[0]
    width = basis.shape[1] // 16

    def send(a, to):
        pairs = [(2 * q + k, 2 * to(q, k) + k) for q in range(16) for k in range(2)]
        return lax.ppermute(a, ("row", "col"), pairs)

    first = lambda a: send(a, lambda q, k: q ^ (1 + k))
    second = lambda a: send(a, lambda q, k: q ^ (2 - k))
    plane = lambda a, d: send(a, lambda q, k: q ^ (4 * d))
    swap = lambda a: lax.ppermute(a, "col", [(0, 1), (1, 0)])
    join = lambda *a: jnp.concatenate(a, axis=0)
    ids = lambda *v: jnp.stack(v).astype(jnp.int32)

    def after(a, *others):
        return lax.optimization_barrier((a, *others))[0]

    near, far = 1 + c, 2 - c

    own, other = split_spins(ids(c), orbitals)
    other = swap(other)
    block = join(own, other)
    rows = jnp.where(c == 0, block, join(other, own))
    block, rows = lax.optimization_barrier((block, rows))
    x0 = first(block)
    z8 = plane(block, 2)
    p0 = join_blocks(block, x0)
    y0 = second(p0)
    z12 = plane(z8, 1)
    x8 = first(z8)
    zp = plane(join_blocks(p0, y0), 1)
    x12 = first(z12)
    p8 = join_blocks(z8, x8)
    y8 = second(p8)
    p12 = join_blocks(z12, x12)
    y12 = second(p12)
    kernel_other = swap(after(kernel, x8))
    tiles = turn_tiles(
        ids(*[r ^ (near * a) ^ (far * b) ^ (4 * k) for a in (1, 0) for b in (1, 0) for k in range(4)]),
        after(basis, x12), width,
    )

    around = lambda base: [base ^ d for d in (0, near, far, 3)]
    halves = (rows, kernel, kernel_other)
    acc = apply_blocks(ids(*around(r), *around(r ^ 8)), *halves, [p0, y0, p8, y8], None, F32, 20)
    applied = apply_blocks(ids(*around(r ^ 4), *around(r ^ 12)), *halves, [zp, p12, y12], acc, BF16, 1)

    n = 4 * width
    (send_a,) = project(0, tiles, applied, [(n, BF16)])
    send_b, keep_a, keep_b = project(n, tiles, applied, [(n, BF16), (n, F32), (n, F32)])
    got_a, got_b = first(send_a), first(send_b)
    rest = second((keep_a + got_a.astype(F32)).astype(BF16)).astype(F32) + (keep_b + got_b.astype(F32))
    result = rest[:width]
    for k in (1, 2, 3):
        result = result + plane(rest[k * width : (k + 1) * width].astype(BF16), k).astype(F32)
    partner = swap(result)
    return jnp.where(
        c == 0, jnp.stack([result, partner], axis=1), jnp.stack([partner, result], axis=1)
    )


def solution(mesh):
    box = dict(mesh.shape) == {"row": 16, "col": 2}
    return jax.shard_map(
        box_body if box else general_body,
        mesh=mesh,
        in_specs=(P(("row", "col"), None, None), P("row", "col"), P("row", None)),
        out_specs=P("row", None, None),
        check_vma=False,
    )
```

```python
import functools

import jax
import jax.numpy as jnp
from jax import lax
from jax.experimental import pallas as pl
from jax.experimental.pallas import tpu as pltpu
from jax.sharding import PartitionSpec as P

F32 = jnp.float32
BF16 = jnp.bfloat16
VMEM = pl.BlockSpec(memory_space=pltpu.VMEM)
SMEM = pl.BlockSpec(memory_space=pltpu.SMEM)
ANY = pl.BlockSpec(memory_space=pl.ANY)
LIMIT = 40 * 1024 * 1024


def general_body(orbitals, kernel, basis):
    row_orbitals = lax.all_gather(orbitals, "col", axis=0, tiled=True)
    point_rows = row_orbitals.shape[0]
    occupied = orbitals.shape[2]
    column_orbitals = lax.all_gather(orbitals, "row", axis=0, tiled=True)
    density = jnp.einsum(
        "psi,qsi->spq", row_orbitals, column_orbitals, preferred_element_type=F32
    )
    weighted = (density * kernel[None].astype(F32)).astype(BF16)
    applied = jnp.einsum(
        "spq,qsi->psi", weighted, column_orbitals, preferred_element_type=F32
    )
    out_rows = basis.shape[1] // lax.axis_size("row")
    summed = lax.psum(applied, "col").astype(BF16)
    flattened = summed.reshape(point_rows, -1)
    result = lax.psum_scatter(
        lax.dot_general(basis, flattened, (((0,), (0,)), ((), ())), preferred_element_type=F32),
        "row",
        scatter_dimension=0,
        tiled=True,
    )
    return result.reshape(out_rows, 2, occupied)


PARAMS = pltpu.CompilerParams(vmem_limit_bytes=LIMIT)


def pin(weight):
    return pl.CostEstimate(flops=weight * 10**9, bytes_accessed=10**6, transcendentals=0)


def tile_at(index, width):
    return pl.ds(pl.multiple_of(index * width, width), width)


def split_kernel(core, orbitals, own, other):
    first_core = core[0] == 0
    zero, one = orbitals[:, 0, :], orbitals[:, 1, :]
    own[...] = jnp.where(first_core, zero, one)
    other[...] = jnp.where(first_core, one, zero)


def split_spins(core, orbitals):
    p, _, i = orbitals.shape
    return pl.pallas_call(
        split_kernel,
        out_shape=[jax.ShapeDtypeStruct((p, i), orbitals.dtype)] * 2,
        in_specs=[SMEM, VMEM],
        out_specs=[VMEM] * 2,
        compiler_params=PARAMS,
    )(core, orbitals)


def join_kernel(*refs):
    out = refs[-1]
    start = 0
    for ref in refs[:-1]:
        out[start : start + ref.shape[0], :] = ref[...]
        start += ref.shape[0]


def join_blocks(*blocks, weight=20):
    rows = sum(block.shape[0] for block in blocks)
    return pl.pallas_call(
        join_kernel,
        out_shape=jax.ShapeDtypeStruct((rows, blocks[0].shape[1]), blocks[0].dtype),
        in_specs=[VMEM] * len(blocks),
        out_specs=VMEM,
        compiler_params=PARAMS,
        cost_estimate=pin(weight),
    )(*blocks)


def turn_kernel(width, ids, basis, out):
    for b in range(out.shape[0] // width):
        out[b * width : (b + 1) * width, :] = basis[:, tile_at(ids[b], width)].T


def turn_tiles(ids, basis, width):
    return pl.pallas_call(
        functools.partial(turn_kernel, width),
        out_shape=jax.ShapeDtypeStruct((ids.shape[0] * width, basis.shape[0]), basis.dtype),
        in_specs=[SMEM, VMEM],
        out_specs=VMEM,
        compiler_params=PARAMS,
    )(ids, basis)


def apply_parts(rows, parts, tile, total):
    for t, ref in enumerate(parts):
        columns = ref[...]
        density = lax.dot_general(
            rows, columns, (((1,), (1,)), ((), ())), preferred_element_type=F32
        )
        weighted = (density * tile(t).astype(F32)).astype(BF16)
        term = jnp.dot(weighted, columns, preferred_element_type=F32)
        total = term if total is None else total + term
    return total


def early_kernel(slots, later, piece, ids, rows, kernel, kernel_other, *refs):
    *parts, out, packed, held, sems = refs
    copies = {}
    for k in range(4):
        at = tile_at(ids[k], 4 * piece)
        copies[k] = [
            pltpu.make_async_copy(ref.at[:, at], held.at[k, h], sems.at[2 * k + h])
            for h, ref in enumerate((kernel, kernel_other))
        ]
        for copy in copies[k]:
            copy.start()

    def halves(k, j):
        for copy in copies.pop(k, ()):
            copy.wait()
        at = tile_at(ids[4 + j], piece)
        return [held[k, h, :, at] for h in range(2)]

    out[...] = apply_parts(
        rows[...], parts, lambda t: jnp.concatenate([half for kj in slots[t] for half in halves(*kj)], axis=1), None
    )
    for t, kj in enumerate(later):
        for h, half in enumerate(halves(*kj)):
            packed[:, (2 * t + h) * piece : (2 * t + h + 1) * piece] = half


def late_kernel(rows, packed, acc, tiles, *refs):
    *parts, out, send = refs
    ends = [0]
    for part in parts:
        ends.append(ends[-1] + part.shape[0])
    total = apply_parts(rows[...], parts, lambda t: packed[:, ends[t] : ends[t + 1]], acc[...])
    result = total.astype(out.dtype)
    out[...] = result
    n = send.shape[0]
    send[...] = jnp.dot(tiles[:n, :], result, preferred_element_type=F32).astype(send.dtype)


def apply_early(ids, rows, kernel, kernel_other, parts, later):
    n, i = rows.shape
    slots = tuple(tuple(part) for _, part in parts)
    return pl.pallas_call(
        functools.partial(early_kernel, slots, tuple(later), n // 2),
        out_shape=[jax.ShapeDtypeStruct((n, i), F32), jax.ShapeDtypeStruct((n, n * len(later)), BF16)],
        in_specs=[SMEM, VMEM, ANY, ANY] + [VMEM] * len(parts),
        out_specs=[VMEM] * 2,
        scratch_shapes=[pltpu.VMEM((4, 2, n, 2 * n), BF16), pltpu.SemaphoreType.DMA((8,))],
        compiler_params=PARAMS,
        cost_estimate=pin(60),
    )(ids, rows, kernel, kernel_other, *[array for array, _ in parts])


def apply_late(rows, packed, acc, tiles, parts):
    n, i = rows.shape
    m = tiles.shape[0] // 4
    return pl.pallas_call(
        late_kernel,
        out_shape=[jax.ShapeDtypeStruct((n, i), BF16), jax.ShapeDtypeStruct((m, i), BF16)],
        in_specs=[VMEM] * (4 + len(parts)),
        out_specs=[VMEM] * 2,
        compiler_params=PARAMS,
        cost_estimate=pin(1),
    )(rows, packed, acc, tiles, *parts)


def project_kernel(start, tiles, applied, *outs):
    for out in outs:
        n = out.shape[0]
        total = jnp.dot(tiles[start : start + n, :], applied[...], preferred_element_type=F32)
        out[...] = total.astype(out.dtype)
        start += n


def project(start, tiles, applied, shapes):
    p, i = applied.shape
    rows = sum(n for n, _ in shapes)
    return pl.pallas_call(
        functools.partial(project_kernel, start),
        out_shape=[jax.ShapeDtypeStruct((n, i), t) for n, t in shapes],
        in_specs=[VMEM, VMEM],
        out_specs=[VMEM] * len(shapes),
        compiler_params=PARAMS,
        cost_estimate=pl.CostEstimate(flops=2 * rows * p * i, bytes_accessed=4 * rows * p, transcendentals=0),
    )(tiles, applied)


def halve_kernel(keep, got, *outs):
    start = 0
    for out in outs:
        m = slice(start, start + out.shape[0])
        start = m.stop
        out[...] = (keep[m, :] + got[m, :].astype(F32)).astype(out.dtype)


def halve(keep, got, shapes):
    return pl.pallas_call(
        halve_kernel,
        out_shape=[jax.ShapeDtypeStruct((n, keep.shape[1]), t) for n, t in shapes],
        in_specs=[VMEM] * 2,
        out_specs=[VMEM] * len(shapes),
        compiler_params=PARAMS,
        cost_estimate=pin(20),
    )(keep, got)


def collect_kernel(start, keep, got, more, *outs):
    at = 0
    for out in outs:
        m, here = slice(start + at, start + at + out.shape[0]), slice(at, at + out.shape[0])
        at = here.stop
        out[...] = (keep[m, :] + got[m, :].astype(F32) + more[here, :].astype(F32)).astype(out.dtype)


def collect(start, keep, got, more, shapes):
    return pl.pallas_call(
        functools.partial(collect_kernel, start),
        out_shape=[jax.ShapeDtypeStruct((n, keep.shape[1]), t) for n, t in shapes],
        in_specs=[VMEM] * 3,
        out_specs=[VMEM] * len(shapes),
        compiler_params=PARAMS,
        cost_estimate=pin(20),
    )(keep, got, more)


def spins_kernel(core, result, partner, out):
    out[:, pl.ds(core[0], 1), :] = result[...][:, None, :]
    out[:, pl.ds(1 - core[0], 1), :] = partner[...][:, None, :]


def both_spins(core, result, partner):
    n, i = result.shape
    return pl.pallas_call(
        spins_kernel,
        out_shape=jax.ShapeDtypeStruct((n, 2, i), F32),
        in_specs=[SMEM, VMEM, VMEM],
        out_specs=VMEM,
        compiler_params=PARAMS,
    )(core, result, partner)


def box_body(orbitals, kernel, basis):
    r = lax.axis_index("row")
    c = lax.axis_index("col")
    piece = orbitals.shape[0]
    width = basis.shape[1] // 16

    def send(a, to):
        pairs = [(2 * q + k, 2 * to(q, k) + k) for q in range(16) for k in range(2)]
        return lax.ppermute(a, ("row", "col"), pairs)

    first = lambda a: send(a, lambda q, k: q ^ (1 + k))
    second = lambda a: send(a, lambda q, k: q ^ (2 - k))
    plane = lambda a, d: send(a, lambda q, k: q ^ (4 * d))
    swap = lambda a: lax.ppermute(a, "col", [(0, 1), (1, 0)])
    join = lambda *a: jnp.concatenate(a, axis=0)
    ids = lambda *v: jnp.stack(v).astype(jnp.int32)

    def after(a, *others):
        return lax.optimization_barrier((a, *others))[0]

    near, far = 1 + c, 2 - c

    own, other = split_spins(ids(c), orbitals)
    other = swap(other)
    block = join(own, other)
    rows = jnp.where(c == 0, block, join(other, own))
    block, rows = lax.optimization_barrier((block, rows))
    x0 = first(block)
    z8 = plane(block, 2)
    p0 = join_blocks(block, x0)
    y0 = second(p0)
    whole = join_blocks(p0, y0)
    z4 = plane(whole, 1)
    z12 = plane(z8, 1)
    x8 = first(z8)
    x12 = first(z12)
    p8 = join_blocks(after(z8, whole), x8, weight=6)
    y8 = second(p8)
    p12 = join_blocks(z12, x12)
    y12 = second(p12)

    kernel_other = swap(after(kernel, x12))
    order = (1, 2, 0, 3)
    tiles = turn_tiles(
        ids(*[r ^ (near * a) ^ (far * b) ^ (4 * k) for a in (1, 0) for b in (1, 0) for k in order]),
        after(basis, x12), width,
    )
    places = ids(*[(r // 4) ^ k for k in range(4)], *[(r & 3) ^ d for d in (0, near, far, 3)])
    at = lambda k, *js: [(k, j) for j in js]
    acc, packed = apply_early(
        places, rows, kernel, kernel_other,
        [(p0, at(0, 0, 1)), (y0, at(0, 2, 3)), (p8, at(2, 0, 1)), (y8, at(2, 2, 3)), (p12, at(3, 0, 1))],
        at(3, 2, 3) + at(1, 0, 1, 2, 3),
    )
    applied, send_a = apply_late(rows, packed, acc, tiles, [y12, z4])

    n, pair = 4 * width, 2 * width
    send_b, keep_a, keep_b = project(n, tiles, applied, [(n, BF16), (n, F32), (n, F32)])
    got_a, got_b = first(send_a), first(send_b)
    high, low = halve(keep_a, got_a, [(pair, BF16)] * 2)
    got_high, got_low = second(high), second(low)
    to_0, to_1 = collect(0, keep_b, got_b, got_high, [(width, BF16)] * 2)
    from_0, from_1 = plane(to_0, order[0]), plane(to_1, order[1])
    rest, to_3 = collect(pair, keep_b, got_b, got_low, [(width, F32), (width, BF16)])
    result = rest + plane(to_3, order[3]).astype(F32) + from_0.astype(F32) + from_1.astype(F32)
    return both_spins(ids(c), result, swap(result))


def solution(mesh):
    box = dict(mesh.shape) == {"row": 16, "col": 2}
    return jax.shard_map(
        box_body if box else general_body,
        mesh=mesh,
        in_specs=(P(("row", "col"), None, None), P("row", "col"), P("row", None)),
        out_specs=P("row", None, None),
        check_vma=False,
    )
```

```python
import functools

import jax
import jax.numpy as jnp
from jax import lax
from jax.experimental import pallas as pl
from jax.experimental.pallas import tpu as pltpu
from jax.sharding import PartitionSpec as P

F32 = jnp.float32
BF16 = jnp.bfloat16
VMEM = pl.BlockSpec(memory_space=pltpu.VMEM)
SMEM = pl.BlockSpec(memory_space=pltpu.SMEM)
ANY = pl.BlockSpec(memory_space=pl.ANY)
LIMIT = 40 * 1024 * 1024


def general_body(orbitals, kernel, basis):
    row_orbitals = lax.all_gather(orbitals, "col", axis=0, tiled=True)
    point_rows = row_orbitals.shape[0]
    occupied = orbitals.shape[2]
    column_orbitals = lax.all_gather(orbitals, "row", axis=0, tiled=True)
    density = jnp.einsum(
        "psi,qsi->spq", row_orbitals, column_orbitals, preferred_element_type=F32
    )
    weighted = (density * kernel[None].astype(F32)).astype(BF16)
    applied = jnp.einsum(
        "spq,qsi->psi", weighted, column_orbitals, preferred_element_type=F32
    )
    out_rows = basis.shape[1] // lax.axis_size("row")
    summed = lax.psum(applied, "col").astype(BF16)
    flattened = summed.reshape(point_rows, -1)
    result = lax.psum_scatter(
        lax.dot_general(basis, flattened, (((0,), (0,)), ((), ())), preferred_element_type=F32),
        "row",
        scatter_dimension=0,
        tiled=True,
    )
    return result.reshape(out_rows, 2, occupied)


PARAMS = pltpu.CompilerParams(vmem_limit_bytes=LIMIT)


def pin(weight):
    return pl.CostEstimate(flops=weight * 10**9, bytes_accessed=10**6, transcendentals=0)


def tile_at(index, width):
    return pl.ds(pl.multiple_of(index * width, width), width)


def split_kernel(core, orbitals, own, other):
    first_core = core[0] == 0
    zero, one = orbitals[:, 0, :], orbitals[:, 1, :]
    own[...] = jnp.where(first_core, zero, one)
    other[...] = jnp.where(first_core, one, zero)


def split_spins(core, orbitals, weight):
    p, _, i = orbitals.shape
    return pl.pallas_call(
        split_kernel,
        out_shape=[jax.ShapeDtypeStruct((p, i), orbitals.dtype)] * 2,
        in_specs=[SMEM, VMEM],
        out_specs=[VMEM] * 2,
        compiler_params=PARAMS,
        cost_estimate=pin(weight),
    )(core, orbitals)


def join_kernel(*refs):
    out = refs[-1]
    start = 0
    for ref in refs[:-1]:
        out[start : start + ref.shape[0], :] = ref[...]
        start += ref.shape[0]


def join_blocks(*blocks, weight=20):
    rows = sum(block.shape[0] for block in blocks)
    return pl.pallas_call(
        join_kernel,
        out_shape=jax.ShapeDtypeStruct((rows, blocks[0].shape[1]), blocks[0].dtype),
        in_specs=[VMEM] * len(blocks),
        out_specs=VMEM,
        compiler_params=PARAMS,
        cost_estimate=pin(weight),
    )(*blocks)


def turn_kernel(width, ids, basis, out):
    for b in range(out.shape[0] // width):
        out[b * width : (b + 1) * width, :] = basis[:, tile_at(ids[b], width)].T


def turn_tiles(ids, basis, width):
    return pl.pallas_call(
        functools.partial(turn_kernel, width),
        out_shape=jax.ShapeDtypeStruct((ids.shape[0] * width, basis.shape[0]), basis.dtype),
        in_specs=[SMEM, VMEM],
        out_specs=VMEM,
        compiler_params=PARAMS,
    )(ids, basis)


def apply_parts(rows, parts, tile, total):
    for t, ref in enumerate(parts):
        columns = ref[...]
        density = lax.dot_general(
            rows, columns, (((1,), (1,)), ((), ())), preferred_element_type=F32
        )
        weighted = (density * tile(t).astype(F32)).astype(BF16)
        term = jnp.dot(weighted, columns, preferred_element_type=F32)
        total = term if total is None else total + term
    return total


def early_kernel(slots, later, piece, ids, rows, kernel, kernel_other, *refs):
    *parts, out, packed, held, sems = refs
    copies = {}
    for k in range(4):
        at = tile_at(ids[k], 4 * piece)
        copies[k] = [
            pltpu.make_async_copy(ref.at[:, at], held.at[k, h], sems.at[2 * k + h])
            for h, ref in enumerate((kernel, kernel_other))
        ]
        for copy in copies[k]:
            copy.start()

    def halves(k, j):
        for copy in copies.pop(k, ()):
            copy.wait()
        at = tile_at(ids[4 + j], piece)
        return [held[k, h, :, at] for h in range(2)]

    out[...] = apply_parts(
        rows[...], parts, lambda t: jnp.concatenate([half for kj in slots[t] for half in halves(*kj)], axis=1), None
    )
    for t, kj in enumerate(later):
        for h, half in enumerate(halves(*kj)):
            packed[:, (2 * t + h) * piece : (2 * t + h + 1) * piece] = half


def late_kernel(rows, packed, acc, tiles, *refs):
    *parts, out, send = refs
    ends = [0]
    for part in parts:
        ends.append(ends[-1] + part.shape[0])
    total = apply_parts(rows[...], parts, lambda t: packed[:, ends[t] : ends[t + 1]], acc[...])
    result = total.astype(out.dtype)
    out[...] = result
    n = send.shape[0]
    send[...] = jnp.dot(tiles[:n, :], result, preferred_element_type=F32).astype(send.dtype)


def apply_early(ids, rows, kernel, kernel_other, parts, later):
    n, i = rows.shape
    slots = tuple(tuple(part) for _, part in parts)
    return pl.pallas_call(
        functools.partial(early_kernel, slots, tuple(later), n // 2),
        out_shape=[jax.ShapeDtypeStruct((n, i), F32), jax.ShapeDtypeStruct((n, n * len(later)), BF16)],
        in_specs=[SMEM, VMEM, ANY, ANY] + [VMEM] * len(parts),
        out_specs=[VMEM] * 2,
        scratch_shapes=[pltpu.VMEM((4, 2, n, 2 * n), BF16), pltpu.SemaphoreType.DMA((8,))],
        compiler_params=PARAMS,
        cost_estimate=pin(60),
    )(ids, rows, kernel, kernel_other, *[array for array, _ in parts])


def apply_late(rows, packed, acc, tiles, parts):
    n, i = rows.shape
    m = tiles.shape[0] // 4
    return pl.pallas_call(
        late_kernel,
        out_shape=[jax.ShapeDtypeStruct((n, i), BF16), jax.ShapeDtypeStruct((m, i), BF16)],
        in_specs=[VMEM] * (4 + len(parts)),
        out_specs=[VMEM] * 2,
        compiler_params=PARAMS,
        cost_estimate=pin(1),
    )(rows, packed, acc, tiles, *parts)


def project_kernel(start, tiles, applied, *outs):
    for out in outs:
        n = out.shape[0]
        total = jnp.dot(tiles[start : start + n, :], applied[...], preferred_element_type=F32)
        out[...] = total.astype(out.dtype)
        start += n


def project(start, tiles, applied, shapes):
    p, i = applied.shape
    rows = sum(n for n, _ in shapes)
    return pl.pallas_call(
        functools.partial(project_kernel, start),
        out_shape=[jax.ShapeDtypeStruct((n, i), t) for n, t in shapes],
        in_specs=[VMEM, VMEM],
        out_specs=[VMEM] * len(shapes),
        compiler_params=PARAMS,
        cost_estimate=pl.CostEstimate(flops=2 * rows * p * i, bytes_accessed=4 * rows * p, transcendentals=0),
    )(tiles, applied)


def halve_kernel(keep, got, *outs):
    start = 0
    for out in outs:
        m = slice(start, start + out.shape[0])
        start = m.stop
        out[...] = (keep[m, :] + got[m, :].astype(F32)).astype(out.dtype)


def halve(keep, got, shapes):
    return pl.pallas_call(
        halve_kernel,
        out_shape=[jax.ShapeDtypeStruct((n, keep.shape[1]), t) for n, t in shapes],
        in_specs=[VMEM] * 2,
        out_specs=[VMEM] * len(shapes),
        compiler_params=PARAMS,
        cost_estimate=pin(20),
    )(keep, got)


def collect_kernel(start, keep, got, more, *outs):
    at = 0
    for out in outs:
        m, here = slice(start + at, start + at + out.shape[0]), slice(at, at + out.shape[0])
        at = here.stop
        out[...] = (keep[m, :] + got[m, :].astype(F32) + more[here, :].astype(F32)).astype(out.dtype)


def collect(start, keep, got, more, shapes):
    return pl.pallas_call(
        functools.partial(collect_kernel, start),
        out_shape=[jax.ShapeDtypeStruct((n, keep.shape[1]), t) for n, t in shapes],
        in_specs=[VMEM] * 3,
        out_specs=[VMEM] * len(shapes),
        compiler_params=PARAMS,
        cost_estimate=pin(20),
    )(keep, got, more)


def spins_kernel(core, result, partner, out):
    out[:, pl.ds(core[0], 1), :] = result[...][:, None, :]
    out[:, pl.ds(1 - core[0], 1), :] = partner[...][:, None, :]


def both_spins(core, result, partner):
    n, i = result.shape
    return pl.pallas_call(
        spins_kernel,
        out_shape=jax.ShapeDtypeStruct((n, 2, i), F32),
        in_specs=[SMEM, VMEM, VMEM],
        out_specs=VMEM,
        compiler_params=PARAMS,
    )(core, result, partner)


def box_body(orbitals, kernel, basis):
    r = lax.axis_index("row")
    c = lax.axis_index("col")
    piece = orbitals.shape[0]
    width = basis.shape[1] // 16

    def send(a, to):
        pairs = [(2 * q + k, 2 * to(q, k) + k) for q in range(16) for k in range(2)]
        return lax.ppermute(a, ("row", "col"), pairs)

    first = lambda a: send(a, lambda q, k: q ^ (1 + k))
    second = lambda a: send(a, lambda q, k: q ^ (2 - k))
    plane = lambda a, d: send(a, lambda q, k: q ^ (4 * d))
    swap = lambda a: lax.ppermute(a, "col", [(0, 1), (1, 0)])
    join = lambda *a: jnp.concatenate(a, axis=0)
    ids = lambda *v: jnp.stack(v).astype(jnp.int32)

    def after(a, *others):
        return lax.optimization_barrier((a, *others))[0]

    near, far = 1 + c, 2 - c

    core = ids(c)
    raw8 = plane(orbitals, 2)
    own, other = split_spins(core, orbitals, 0)
    other = swap(other)
    block = join(own, other)
    rows = jnp.where(c == 0, block, join(other, own))
    block, rows = lax.optimization_barrier((block, rows))

    own8, other8 = split_spins(core, raw8, 20)
    x0 = first(block)
    p0 = join_blocks(after(block, own8), x0, weight=6)
    y0 = second(p0)
    whole = join_blocks(p0, y0)
    raw12 = plane(after(raw8, p0), 1)
    z8 = join_blocks(own8, swap(other8), weight=2)
    own12, other12 = split_spins(core, raw12, 6)
    z12 = join_blocks(own12, swap(other12), weight=6)
    x8 = first(z8)
    z4 = plane(whole, 1)
    x12 = first(after(z12, whole))
    p8 = join_blocks(after(z8, whole), x8, weight=6)
    p12 = join_blocks(z12, x12)
    y8 = second(p8)
    y12 = second(p12)

    kernel_other = swap(after(kernel, x12))
    order = (1, 2, 0, 3)
    tiles = turn_tiles(
        ids(*[r ^ (near * a) ^ (far * b) ^ (4 * k) for a in (1, 0) for b in (1, 0) for k in order]),
        after(basis, x12), width,
    )
    places = ids(*[(r // 4) ^ k for k in range(4)], *[(r & 3) ^ d for d in (0, near, far, 3)])
    at = lambda k, *js: [(k, j) for j in js]
    acc, packed = apply_early(
        places, rows, kernel, kernel_other,
        [(p0, at(0, 0, 1)), (y0, at(0, 2, 3)), (p8, at(2, 0, 1)), (y8, at(2, 2, 3)), (p12, at(3, 0, 1))],
        at(3, 2, 3) + at(1, 0, 1, 2, 3),
    )
    applied, send_a = apply_late(rows, packed, acc, tiles, [y12, z4])

    n, pair = 4 * width, 2 * width
    (send_b,) = project(n, tiles, applied, [(n, BF16)])
    keep_a, keep_b = project(2 * n, tiles, applied, [(n, F32), (n, F32)])
    got_a, got_b = first(send_a), first(send_b)
    high, low = halve(keep_a, got_a, [(pair, BF16)] * 2)
    got_high, got_low = second(high), second(low)
    to_0, to_1 = collect(0, keep_b, got_b, got_high, [(width, BF16)] * 2)
    from_0, from_1 = plane(to_0, order[0]), plane(to_1, order[1])
    rest, to_3 = collect(pair, keep_b, got_b, got_low, [(width, F32), (width, BF16)])
    result = rest + plane(to_3, order[3]).astype(F32) + from_0.astype(F32) + from_1.astype(F32)
    return both_spins(core, result, swap(result))


def solution(mesh):
    box = dict(mesh.shape) == {"row": 16, "col": 2}
    return jax.shard_map(
        box_body if box else general_body,
        mesh=mesh,
        in_specs=(P(("row", "col"), None, None), P("row", "col"), P("row", None)),
        out_specs=P("row", None, None),
        check_vma=False,
    )
```

```python
import functools

import jax
import jax.numpy as jnp
from jax import lax
from jax.experimental import pallas as pl
from jax.experimental.pallas import tpu as pltpu
from jax.sharding import PartitionSpec as P

F32 = jnp.float32
BF16 = jnp.bfloat16
VMEM = pl.BlockSpec(memory_space=pltpu.VMEM)
SMEM = pl.BlockSpec(memory_space=pltpu.SMEM)
ANY = pl.BlockSpec(memory_space=pl.ANY)
LIMIT = 40 * 1024 * 1024


def general_body(orbitals, kernel, basis):
    row_orbitals = lax.all_gather(orbitals, "col", axis=0, tiled=True)
    point_rows = row_orbitals.shape[0]
    occupied = orbitals.shape[2]
    column_orbitals = lax.all_gather(orbitals, "row", axis=0, tiled=True)
    density = jnp.einsum(
        "psi,qsi->spq", row_orbitals, column_orbitals, preferred_element_type=F32
    )
    weighted = (density * kernel[None].astype(F32)).astype(BF16)
    applied = jnp.einsum(
        "spq,qsi->psi", weighted, column_orbitals, preferred_element_type=F32
    )
    out_rows = basis.shape[1] // lax.axis_size("row")
    summed = lax.psum(applied, "col").astype(BF16)
    flattened = summed.reshape(point_rows, -1)
    result = lax.psum_scatter(
        lax.dot_general(basis, flattened, (((0,), (0,)), ((), ())), preferred_element_type=F32),
        "row",
        scatter_dimension=0,
        tiled=True,
    )
    return result.reshape(out_rows, 2, occupied)


PARAMS = pltpu.CompilerParams(vmem_limit_bytes=LIMIT)


def pin(weight):
    return pl.CostEstimate(flops=weight * 10**9, bytes_accessed=10**6, transcendentals=0)


def tile_at(index, width):
    return pl.ds(pl.multiple_of(index * width, width), width)


def split_kernel(core, orbitals, own, other):
    first_core = core[0] == 0
    zero, one = orbitals[:, 0, :], orbitals[:, 1, :]
    own[...] = jnp.where(first_core, zero, one)
    other[...] = jnp.where(first_core, one, zero)


def split_spins(core, orbitals, weight):
    p, _, i = orbitals.shape
    return pl.pallas_call(
        split_kernel,
        out_shape=[jax.ShapeDtypeStruct((p, i), orbitals.dtype)] * 2,
        in_specs=[SMEM, VMEM],
        out_specs=[VMEM] * 2,
        compiler_params=PARAMS,
        cost_estimate=pin(weight),
    )(core, orbitals)


def join_kernel(*refs):
    out = refs[-1]
    start = 0
    for ref in refs[:-1]:
        out[start : start + ref.shape[0], :] = ref[...]
        start += ref.shape[0]


def join_blocks(*blocks, weight=20):
    rows = sum(block.shape[0] for block in blocks)
    return pl.pallas_call(
        join_kernel,
        out_shape=jax.ShapeDtypeStruct((rows, blocks[0].shape[1]), blocks[0].dtype),
        in_specs=[VMEM] * len(blocks),
        out_specs=VMEM,
        compiler_params=PARAMS,
        cost_estimate=pin(weight),
    )(*blocks)


def turn_kernel(width, ids, basis, out):
    for b in range(out.shape[0] // width):
        out[b * width : (b + 1) * width, :] = basis[:, tile_at(ids[b], width)].T


def turn_tiles(ids, basis, width):
    return pl.pallas_call(
        functools.partial(turn_kernel, width),
        out_shape=jax.ShapeDtypeStruct((ids.shape[0] * width, basis.shape[0]), basis.dtype),
        in_specs=[SMEM, VMEM],
        out_specs=VMEM,
        compiler_params=PARAMS,
    )(ids, basis)


def apply_parts(rows, parts, tile, total):
    for t, ref in enumerate(parts):
        columns = ref[...]
        density = lax.dot_general(
            rows, columns, (((1,), (1,)), ((), ())), preferred_element_type=F32
        )
        weighted = (density * tile(t).astype(F32)).astype(BF16)
        term = jnp.dot(weighted, columns, preferred_element_type=F32)
        total = term if total is None else total + term
    return total


def early_kernel(slots, later, piece, ids, rows, kernel, kernel_other, *refs):
    *parts, out, packed, held, sems = refs
    copies = {}
    for k in range(4):
        at = tile_at(ids[k], 4 * piece)
        copies[k] = [
            pltpu.make_async_copy(ref.at[:, at], held.at[k, h], sems.at[2 * k + h])
            for h, ref in enumerate((kernel, kernel_other))
        ]
        for copy in copies[k]:
            copy.start()

    def halves(k, j):
        for copy in copies.pop(k, ()):
            copy.wait()
        at = tile_at(ids[4 + j], piece)
        return [held[k, h, :, at] for h in range(2)]

    out[...] = apply_parts(
        rows[...], parts, lambda t: jnp.concatenate([half for kj in slots[t] for half in halves(*kj)], axis=1), None
    )
    for t, kj in enumerate(later):
        for h, half in enumerate(halves(*kj)):
            packed[:, (2 * t + h) * piece : (2 * t + h + 1) * piece] = half


def late_kernel(rows, packed, acc, tiles, *refs):
    *parts, out, send = refs
    ends = [0]
    for part in parts:
        ends.append(ends[-1] + part.shape[0])
    total = apply_parts(rows[...], parts, lambda t: packed[:, ends[t] : ends[t + 1]], acc[...])
    result = total.astype(out.dtype)
    out[...] = result
    n = send.shape[0]
    send[...] = jnp.dot(tiles[:n, :], result, preferred_element_type=F32).astype(send.dtype)


def apply_early(ids, rows, kernel, kernel_other, parts, later):
    n, i = rows.shape
    slots = tuple(tuple(part) for _, part in parts)
    return pl.pallas_call(
        functools.partial(early_kernel, slots, tuple(later), n // 2),
        out_shape=[jax.ShapeDtypeStruct((n, i), F32), jax.ShapeDtypeStruct((n, n * len(later)), BF16)],
        in_specs=[SMEM, VMEM, ANY, ANY] + [VMEM] * len(parts),
        out_specs=[VMEM] * 2,
        scratch_shapes=[pltpu.VMEM((4, 2, n, 2 * n), BF16), pltpu.SemaphoreType.DMA((8,))],
        compiler_params=PARAMS,
        cost_estimate=pin(60),
    )(ids, rows, kernel, kernel_other, *[array for array, _ in parts])


def apply_late(rows, packed, acc, tiles, parts):
    n, i = rows.shape
    m = tiles.shape[0] // 4
    return pl.pallas_call(
        late_kernel,
        out_shape=[jax.ShapeDtypeStruct((n, i), BF16), jax.ShapeDtypeStruct((m, i), BF16)],
        in_specs=[VMEM] * (4 + len(parts)),
        out_specs=[VMEM] * 2,
        compiler_params=PARAMS,
        cost_estimate=pin(1),
    )(rows, packed, acc, tiles, *parts)


def project_kernel(start, tiles, applied, *outs):
    for out in outs:
        n = out.shape[0]
        total = jnp.dot(tiles[start : start + n, :], applied[...], preferred_element_type=F32)
        out[...] = total.astype(out.dtype)
        start += n


def project(start, tiles, applied, shapes):
    p, i = applied.shape
    rows = sum(n for n, _ in shapes)
    return pl.pallas_call(
        functools.partial(project_kernel, start),
        out_shape=[jax.ShapeDtypeStruct((n, i), t) for n, t in shapes],
        in_specs=[VMEM, VMEM],
        out_specs=[VMEM] * len(shapes),
        compiler_params=PARAMS,
        cost_estimate=pl.CostEstimate(flops=2 * rows * p * i, bytes_accessed=4 * rows * p, transcendentals=0),
    )(tiles, applied)


def halve_kernel(keep, got, *outs):
    start = 0
    for out in outs:
        m = slice(start, start + out.shape[0])
        start = m.stop
        out[...] = (keep[m, :] + got[m, :].astype(F32)).astype(out.dtype)


def halve(keep, got, shapes):
    return pl.pallas_call(
        halve_kernel,
        out_shape=[jax.ShapeDtypeStruct((n, keep.shape[1]), t) for n, t in shapes],
        in_specs=[VMEM] * 2,
        out_specs=[VMEM] * len(shapes),
        compiler_params=PARAMS,
        cost_estimate=pin(20),
    )(keep, got)


def collect_kernel(start, keep, got, more, *outs):
    at = 0
    for out in outs:
        m, here = slice(start + at, start + at + out.shape[0]), slice(at, at + out.shape[0])
        at = here.stop
        out[...] = (keep[m, :] + got[m, :].astype(F32) + more[here, :].astype(F32)).astype(out.dtype)


def collect(start, keep, got, more, shapes):
    return pl.pallas_call(
        functools.partial(collect_kernel, start),
        out_shape=[jax.ShapeDtypeStruct((n, keep.shape[1]), t) for n, t in shapes],
        in_specs=[VMEM] * 3,
        out_specs=[VMEM] * len(shapes),
        compiler_params=PARAMS,
        cost_estimate=pin(20),
    )(keep, got, more)


def spins_kernel(core, result, partner, out):
    out[:, pl.ds(core[0], 1), :] = result[...][:, None, :]
    out[:, pl.ds(1 - core[0], 1), :] = partner[...][:, None, :]


def both_spins(core, result, partner):
    n, i = result.shape
    return pl.pallas_call(
        spins_kernel,
        out_shape=jax.ShapeDtypeStruct((n, 2, i), F32),
        in_specs=[SMEM, VMEM, VMEM],
        out_specs=VMEM,
        compiler_params=PARAMS,
    )(core, result, partner)


def box_body(orbitals, kernel, basis):
    r = lax.axis_index("row")
    c = lax.axis_index("col")
    piece = orbitals.shape[0]
    width = basis.shape[1] // 16

    def send(a, to):
        pairs = [(2 * q + k, 2 * to(q, k) + k) for q in range(16) for k in range(2)]
        return lax.ppermute(a, ("row", "col"), pairs)

    first = lambda a: send(a, lambda q, k: q ^ (1 + k))
    second = lambda a: send(a, lambda q, k: q ^ (2 - k))
    plane = lambda a, d: send(a, lambda q, k: q ^ (4 * d))
    swap = lambda a: lax.ppermute(a, "col", [(0, 1), (1, 0)])
    join = lambda *a: jnp.concatenate(a, axis=0)
    ids = lambda *v: jnp.stack(v).astype(jnp.int32)

    def after(a, *others):
        return lax.optimization_barrier((a, *others))[0]

    near, far = 1 + c, 2 - c

    core = ids(c)
    raw8 = plane(orbitals, 2)
    own, other = split_spins(core, orbitals, 0)
    other = swap(other)
    block = join(own, other)
    rows = jnp.where(c == 0, block, join(other, own))
    block, rows = lax.optimization_barrier((block, rows))

    own8, other8 = split_spins(core, raw8, 20)
    x0 = first(block)
    p0 = join_blocks(after(block, own8), x0, weight=6)
    y0 = second(p0)
    whole = join_blocks(p0, y0)
    raw12 = plane(after(raw8, p0), 1)
    z8 = join_blocks(own8, swap(other8), weight=2)
    own12, other12 = split_spins(core, raw12, 6)
    z12 = join_blocks(own12, swap(other12), weight=6)
    x8 = first(z8)
    z4 = plane(whole, 1)
    x12 = first(after(z12, whole))
    p8 = join_blocks(after(z8, whole), x8)
    p12 = join_blocks(z12, x12)
    y8 = second(p8)
    y12 = second(p12)

    kernel_other = swap(after(kernel, x12))
    order = (1, 2, 0, 3)
    tiles = turn_tiles(
        ids(*[r ^ (near * a) ^ (far * b) ^ (4 * k) for a in (1, 0) for b in (1, 0) for k in order]),
        after(basis, x12), width,
    )
    places = ids(*[(r // 4) ^ k for k in range(4)], *[(r & 3) ^ d for d in (0, near, far, 3)])
    at = lambda k, *js: [(k, j) for j in js]
    acc, packed = apply_early(
        places, rows, kernel, kernel_other,
        [(p0, at(0, 0, 1)), (y0, at(0, 2, 3)), (p8, at(2, 0, 1)), (y8, at(2, 2, 3)), (p12, at(3, 0, 1))],
        at(3, 2, 3) + at(1, 0, 1, 2, 3),
    )
    applied, send_a = apply_late(rows, packed, acc, tiles, [y12, z4])

    n, pair = 4 * width, 2 * width
    (send_b,) = project(n, tiles, applied, [(n, BF16)])
    keep_a, keep_b = project(2 * n, tiles, applied, [(n, F32), (n, F32)])
    got_a, got_b = first(send_a), first(send_b)
    high, low = halve(keep_a, got_a, [(pair, BF16)] * 2)
    got_high, got_low = second(high), second(low)
    to_0, to_1 = collect(0, keep_b, got_b, got_high, [(width, BF16)] * 2)
    from_0, from_1 = plane(to_0, order[0]), plane(to_1, order[1])
    rest, to_3 = collect(pair, keep_b, got_b, got_low, [(width, F32), (width, BF16)])
    result = rest + plane(to_3, order[3]).astype(F32) + from_0.astype(F32) + from_1.astype(F32)
    return both_spins(core, result, swap(result))


def solution(mesh):
    box = dict(mesh.shape) == {"row": 16, "col": 2}
    return jax.shard_map(
        box_body if box else general_body,
        mesh=mesh,
        in_specs=(P(("row", "col"), None, None), P("row", "col"), P("row", None)),
        out_specs=P("row", None, None),
        check_vma=False,
    )
```

```python
import functools

import jax
import jax.numpy as jnp
from jax import lax
from jax.experimental import pallas as pl
from jax.experimental.pallas import tpu as pltpu
from jax.sharding import PartitionSpec as P

F32 = jnp.float32
BF16 = jnp.bfloat16
VMEM = pl.BlockSpec(memory_space=pltpu.VMEM)
SMEM = pl.BlockSpec(memory_space=pltpu.SMEM)
ANY = pl.BlockSpec(memory_space=pl.ANY)
LIMIT = 40 * 1024 * 1024


def general_body(orbitals, kernel, basis):
    row_orbitals = lax.all_gather(orbitals, "col", axis=0, tiled=True)
    point_rows = row_orbitals.shape[0]
    occupied = orbitals.shape[2]
    column_orbitals = lax.all_gather(orbitals, "row", axis=0, tiled=True)
    density = jnp.einsum(
        "psi,qsi->spq", row_orbitals, column_orbitals, preferred_element_type=F32
    )
    weighted = (density * kernel[None].astype(F32)).astype(BF16)
    applied = jnp.einsum(
        "spq,qsi->psi", weighted, column_orbitals, preferred_element_type=F32
    )
    out_rows = basis.shape[1] // lax.axis_size("row")
    summed = lax.psum(applied, "col").astype(BF16)
    flattened = summed.reshape(point_rows, -1)
    result = lax.psum_scatter(
        lax.dot_general(basis, flattened, (((0,), (0,)), ((), ())), preferred_element_type=F32),
        "row",
        scatter_dimension=0,
        tiled=True,
    )
    return result.reshape(out_rows, 2, occupied)


PARAMS = pltpu.CompilerParams(vmem_limit_bytes=LIMIT)


def pin(weight):
    return pl.CostEstimate(flops=weight * 10**9, bytes_accessed=10**6, transcendentals=0)


def tile_at(index, width):
    return pl.ds(pl.multiple_of(index * width, width), width)


def split_kernel(core, orbitals, own, other):
    first_core = core[0] == 0
    zero, one = orbitals[:, 0, :], orbitals[:, 1, :]
    own[...] = jnp.where(first_core, zero, one)
    other[...] = jnp.where(first_core, one, zero)


def split_spins(core, orbitals, weight):
    p, _, i = orbitals.shape
    return pl.pallas_call(
        split_kernel,
        out_shape=[jax.ShapeDtypeStruct((p, i), orbitals.dtype)] * 2,
        in_specs=[SMEM, VMEM],
        out_specs=[VMEM] * 2,
        compiler_params=PARAMS,
        cost_estimate=pin(weight),
    )(core, orbitals)


def join_kernel(*refs):
    out = refs[-1]
    start = 0
    for ref in refs[:-1]:
        out[start : start + ref.shape[0], :] = ref[...]
        start += ref.shape[0]


def join_blocks(*blocks, weight=20):
    rows = sum(block.shape[0] for block in blocks)
    return pl.pallas_call(
        join_kernel,
        out_shape=jax.ShapeDtypeStruct((rows, blocks[0].shape[1]), blocks[0].dtype),
        in_specs=[VMEM] * len(blocks),
        out_specs=VMEM,
        compiler_params=PARAMS,
        cost_estimate=pin(weight),
    )(*blocks)


def turn_kernel(width, ids, basis, out):
    for b in range(out.shape[0] // width):
        out[b * width : (b + 1) * width, :] = basis[:, tile_at(ids[b], width)].T


def turn_tiles(ids, basis, width):
    return pl.pallas_call(
        functools.partial(turn_kernel, width),
        out_shape=jax.ShapeDtypeStruct((ids.shape[0] * width, basis.shape[0]), basis.dtype),
        in_specs=[SMEM, VMEM],
        out_specs=VMEM,
        compiler_params=PARAMS,
    )(ids, basis)


def apply_parts(rows, parts, tile, total):
    for t, ref in enumerate(parts):
        columns = ref[...]
        density = lax.dot_general(
            rows, columns, (((1,), (1,)), ((), ())), preferred_element_type=F32
        )
        weighted = (density * tile(t).astype(F32)).astype(BF16)
        term = jnp.dot(weighted, columns, preferred_element_type=F32)
        total = term if total is None else total + term
    return total


def early_kernel(slots, later, piece, ids, rows, kernel, kernel_other, *refs):
    *parts, out, packed, held, sems = refs
    copies = {}
    for k in range(4):
        at = tile_at(ids[k], 4 * piece)
        copies[k] = [
            pltpu.make_async_copy(ref.at[:, at], held.at[k, h], sems.at[2 * k + h])
            for h, ref in enumerate((kernel, kernel_other))
        ]
        for copy in copies[k]:
            copy.start()

    def halves(k, j):
        for copy in copies.pop(k, ()):
            copy.wait()
        at = tile_at(ids[4 + j], piece)
        return [held[k, h, :, at] for h in range(2)]

    out[...] = apply_parts(
        rows[...], parts, lambda t: jnp.concatenate([half for kj in slots[t] for half in halves(*kj)], axis=1), None
    )
    for t, kj in enumerate(later):
        for h, half in enumerate(halves(*kj)):
            packed[:, (2 * t + h) * piece : (2 * t + h + 1) * piece] = half


def late_kernel(rows, packed, acc, tiles, *refs):
    *parts, out, send = refs
    ends = [0]
    for part in parts:
        ends.append(ends[-1] + part.shape[0])
    total = apply_parts(rows[...], parts, lambda t: packed[:, ends[t] : ends[t + 1]], acc[...])
    result = total.astype(out.dtype)
    out[...] = result
    n = send.shape[0]
    send[...] = jnp.dot(tiles[:n, :], result, preferred_element_type=F32).astype(send.dtype)


def apply_early(ids, rows, kernel, kernel_other, parts, later):
    n, i = rows.shape
    slots = tuple(tuple(part) for _, part in parts)
    return pl.pallas_call(
        functools.partial(early_kernel, slots, tuple(later), n // 2),
        out_shape=[jax.ShapeDtypeStruct((n, i), F32), jax.ShapeDtypeStruct((n, n * len(later)), BF16)],
        in_specs=[SMEM, VMEM, ANY, ANY] + [VMEM] * len(parts),
        out_specs=[VMEM] * 2,
        scratch_shapes=[pltpu.VMEM((4, 2, n, 2 * n), BF16), pltpu.SemaphoreType.DMA((8,))],
        compiler_params=PARAMS,
        cost_estimate=pin(60),
    )(ids, rows, kernel, kernel_other, *[array for array, _ in parts])


def apply_late(rows, packed, acc, tiles, parts):
    n, i = rows.shape
    m = tiles.shape[0] // 4
    return pl.pallas_call(
        late_kernel,
        out_shape=[jax.ShapeDtypeStruct((n, i), BF16), jax.ShapeDtypeStruct((m, i), BF16)],
        in_specs=[VMEM] * (4 + len(parts)),
        out_specs=[VMEM] * 2,
        compiler_params=PARAMS,
        cost_estimate=pin(1),
    )(rows, packed, acc, tiles, *parts)


def project_kernel(start, tiles, applied, *outs):
    for out in outs:
        n = out.shape[0]
        total = jnp.dot(tiles[start : start + n, :], applied[...], preferred_element_type=F32)
        out[...] = total.astype(out.dtype)
        start += n


def project(start, tiles, applied, shapes):
    p, i = applied.shape
    rows = sum(n for n, _ in shapes)
    return pl.pallas_call(
        functools.partial(project_kernel, start),
        out_shape=[jax.ShapeDtypeStruct((n, i), t) for n, t in shapes],
        in_specs=[VMEM, VMEM],
        out_specs=[VMEM] * len(shapes),
        compiler_params=PARAMS,
        cost_estimate=pl.CostEstimate(flops=2 * rows * p * i, bytes_accessed=4 * rows * p, transcendentals=0),
    )(tiles, applied)


def halve_kernel(keep, got, *outs):
    start = 0
    for out in outs:
        m = slice(start, start + out.shape[0])
        start = m.stop
        out[...] = (keep[m, :] + got[m, :].astype(F32)).astype(out.dtype)


def halve(keep, got, shapes):
    return pl.pallas_call(
        halve_kernel,
        out_shape=[jax.ShapeDtypeStruct((n, keep.shape[1]), t) for n, t in shapes],
        in_specs=[VMEM] * 2,
        out_specs=[VMEM] * len(shapes),
        compiler_params=PARAMS,
        cost_estimate=pin(20),
    )(keep, got)


def collect_kernel(start, keep, got, more, *outs):
    at = 0
    for out in outs:
        m, here = slice(start + at, start + at + out.shape[0]), slice(at, at + out.shape[0])
        at = here.stop
        out[...] = (keep[m, :] + got[m, :].astype(F32) + more[here, :].astype(F32)).astype(out.dtype)


def collect(start, keep, got, more, shapes):
    return pl.pallas_call(
        functools.partial(collect_kernel, start),
        out_shape=[jax.ShapeDtypeStruct((n, keep.shape[1]), t) for n, t in shapes],
        in_specs=[VMEM] * 3,
        out_specs=[VMEM] * len(shapes),
        compiler_params=PARAMS,
        cost_estimate=pin(20),
    )(keep, got, more)


def spins_kernel(core, result, partner, out):
    out[:, pl.ds(core[0], 1), :] = result[...][:, None, :]
    out[:, pl.ds(1 - core[0], 1), :] = partner[...][:, None, :]


def both_spins(core, result, partner):
    n, i = result.shape
    return pl.pallas_call(
        spins_kernel,
        out_shape=jax.ShapeDtypeStruct((n, 2, i), F32),
        in_specs=[SMEM, VMEM, VMEM],
        out_specs=VMEM,
        compiler_params=PARAMS,
    )(core, result, partner)


def box_body(orbitals, kernel, basis):
    r = lax.axis_index("row")
    c = lax.axis_index("col")
    piece = orbitals.shape[0]
    width = basis.shape[1] // 16

    def send(a, to):
        pairs = [(2 * q + k, 2 * to(q, k) + k) for q in range(16) for k in range(2)]
        return lax.ppermute(a, ("row", "col"), pairs)

    first = lambda a: send(a, lambda q, k: q ^ (1 + k))
    second = lambda a: send(a, lambda q, k: q ^ (2 - k))
    plane = lambda a, d: send(a, lambda q, k: q ^ (4 * d))
    swap = lambda a: lax.ppermute(a, "col", [(0, 1), (1, 0)])
    join = lambda *a: jnp.concatenate(a, axis=0)
    ids = lambda *v: jnp.stack(v).astype(jnp.int32)

    def after(a, *others):
        return lax.optimization_barrier((a, *others))[0]

    near, far = 1 + c, 2 - c

    core = ids(c)
    raw8 = plane(orbitals, 2)
    own, other = split_spins(core, orbitals, 0)
    other = swap(other)
    block = join(own, other)
    rows = jnp.where(c == 0, block, join(other, own))
    block, rows = lax.optimization_barrier((block, rows))

    own8, other8 = split_spins(core, raw8, 20)
    x0 = first(block)
    p0 = join_blocks(after(block, own8), x0, weight=6)
    y0 = second(p0)
    whole = join_blocks(p0, y0)
    raw12 = plane(after(raw8, p0), 1)
    z8 = join_blocks(own8, swap(other8), weight=2)
    own12, other12 = split_spins(core, raw12, 6)
    z12 = join_blocks(own12, swap(other12), weight=6)
    x8 = first(z8)
    z4 = plane(whole, 1)
    x12 = first(after(z12, whole))
    p8 = join_blocks(after(z8, whole), x8, weight=6)
    p12 = join_blocks(z12, x12)
    y8 = second(p8)
    y12 = second(p12)

    kernel_other = swap(after(kernel, x0))
    order = (1, 2, 0, 3)
    tiles = turn_tiles(
        ids(*[r ^ (near * a) ^ (far * b) ^ (4 * k) for a in (1, 0) for b in (1, 0) for k in order]),
        after(basis, x12), width,
    )
    places = ids(*[(r // 4) ^ k for k in range(4)], *[(r & 3) ^ d for d in (0, near, far, 3)])
    at = lambda k, *js: [(k, j) for j in js]
    acc, packed = apply_early(
        places, rows, kernel, kernel_other,
        [(p0, at(0, 0, 1)), (y0, at(0, 2, 3)), (p8, at(2, 0, 1)), (y8, at(2, 2, 3)), (p12, at(3, 0, 1))],
        at(3, 2, 3) + at(1, 0, 1, 2, 3),
    )
    applied, send_a = apply_late(rows, packed, acc, tiles, [y12, z4])

    n, pair = 4 * width, 2 * width
    (send_b,) = project(n, tiles, applied, [(n, BF16)])
    keep_a, keep_b = project(2 * n, tiles, applied, [(n, F32), (n, F32)])
    got_a, got_b = first(send_a), first(send_b)
    high, low = halve(keep_a, got_a, [(pair, BF16)] * 2)
    got_high, got_low = second(high), second(low)
    to_0, to_1 = collect(0, keep_b, got_b, got_high, [(width, BF16)] * 2)
    from_0, from_1 = plane(to_0, order[0]), plane(to_1, order[1])
    rest, to_3 = collect(pair, keep_b, got_b, got_low, [(width, F32), (width, BF16)])
    result = rest + plane(to_3, order[3]).astype(F32) + from_0.astype(F32) + from_1.astype(F32)
    return both_spins(core, result, swap(result))


def solution(mesh):
    box = dict(mesh.shape) == {"row": 16, "col": 2}
    return jax.shard_map(
        box_body if box else general_body,
        mesh=mesh,
        in_specs=(P(("row", "col"), None, None), P("row", "col"), P("row", None)),
        out_specs=P("row", None, None),
        check_vma=False,
    )
```
